256 devices in a mesh: cfg: 8 (over x, y_hi), front: 32 (over y_lo, z, core).
Axes of the slice: x: 4, y: 4 (y_hi: 2, y_lo: 2; y = y_hi * 2 + y_lo), z: 8, core: 2. Of those that a mesh axis runs over, the one named last changes fastest.
Arguments:
- parent_tiles: float32 [2048, 256, 256], P(('cfg', 'front')), parts along dimension 0, may hold values from -6 to 6
- parent_mean: float32 [2048, 256], P(('cfg', 'front')), parts along dimension 0, may hold values from -6 to 6
- factor_w: float32 [768, 1024, 256], P(('cfg', 'front')), parts along dimension 0, may hold values from -0.1875 to 0.1875
- diag_inverse: float32 [768, 256, 256], P(('cfg', 'front')), parts along dimension 0, may hold values from -6 to 6
- own_mean: float32 [768, 256], P(('cfg', 'front')), parts along dimension 0, may hold values from -6 to 6
- config_weight: float32 [8], P('cfg'), parts along dimension 0, may hold values from 0.2 to 2
- need_owner: int32 [1536, 1], replicated, may hold values from 0 to 31; in each aligned block of 48 rows (0 to 47, 48 to 95, ...) at most 2 rows name the same one
- need_local: int32 [1536], replicated, may hold values from 0 to 7
Outputs:
- sigma_pj: float32 [768, 1024, 256], P(('cfg', 'front')), parts along dimension 0
- sigma_jj: float32 [768, 256, 256], P(('cfg', 'front')), parts along dimension 0
- weighted_variance: float32 [768, 256], P(('cfg', 'front')), parts along dimension 0
- weighted_mean: float32 [768, 256], P(('cfg', 'front')), parts along dimension 0
The draws below stay inside these ranges and needn't reach their ends.
There are 8 independent parts, one for each index of `cfg`. The reference program is written for one: setup_inputs(seed, part) draws one part's arguments, and reference() takes and returns one part's arrays. A program takes and returns all parts, laid end to end along the dimension named above; an argument that names none is the same for every part. Nothing has to cross between parts.
Inputs may be any that keep to these rules, and one draw needn't show every extreme that they name: `need_owner`: in each aligned block of 48 reads (the children of one index of front) at most 2 reads name one owner; some block reaches 2.
All inputs are finite; a program needn't handle non-finite values.
Results may differ from the reference program's by a relative error of at most 0.000094.
Values sent between devices are 32-bit elements; how exact they have to be, the bound alone decides.
A program may use at most 128 MiB of HBM per device.

```python
import math
import jax
import jax.numpy as jnp
import numpy as np
from jax import lax

TILE = 256
BJ = 256
KP = 4
CH_DEV = 3
NEED_DEV = 48
CAP = 2
PT_DEV = 8
CHILDREN = 96
PTILES = 256
ITEMS = 1536
N_FRONT = 32


def place_ends(entries, own_key, smallest, top_value):
    shape = entries.shape
    place = [jax.random.randint(jax.random.fold_in(own_key, axis), (), 0, shape[axis]) for axis in range(len(shape))]
    entries = entries.at[tuple(place)].set(smallest)
    longest = shape.index(max(shape))
    place[longest] = (place[longest] + 1) % shape[longest]
    return entries.at[tuple(place)].set(top_value)


def shard_levels(key, dims, pieces, smallest, top_value):
    level = 1.0
    for axis_at, parts in pieces:
        steps = jax.random.uniform(jax.random.fold_in(jax.random.fold_in(key, 6), axis_at), (parts,), jnp.float32, smallest / len(pieces), top_value / len(pieces))
        level = level * jnp.repeat(jnp.exp(steps), dims[axis_at] // parts).reshape((-1,) + (1,) * (len(dims) - 1 - axis_at))
    return level


def routed_block(rng, own, number, rows, count, top, bound, lean):
    order = jax.random.permutation(rng, count)
    crowded, usual = load_shares(count, rows * top, bound, lean, True), load_shares(count, rows * top, bound, lean, False)
    places = jnp.arange(count)

    def named(tallies, offset_by):
        used = int((tallies > 0).sum())
        fixed = max(1, used // 4)
        moved = fixed + (places - fixed + offset_by * (used - fixed)) % max(1, count - fixed)
        return jnp.zeros((count,), jnp.int32).at[order[jnp.where(places < fixed, places, moved)]].set(jnp.asarray(tallies, jnp.int32))

    tallies = jnp.where(number % 4 == 0, named(crowded, number // 4), named(usual, number - number // 4 - 1))
    mixed = jax.random.permutation(jax.random.fold_in(own, 3), count)
    giver, taker = mixed[0:count // 2 * 2:2], mixed[1:count // 2 * 2:2]
    margin = jnp.minimum(tallies[giver] - 1, bound - tallies[taker]) // 2
    margin = jnp.where((giver == order[0]) | (taker == order[0]) | (tallies[taker] == 0), 0, jnp.maximum(margin, 0))
    moved = jax.random.randint(jax.random.fold_in(own, 4), (count // 2,), 0, 1 << 20) % (margin + 1)
    tallies = tallies.at[giver].add(-moved).at[taker].add(moved)
    items = jnp.searchsorted(jnp.cumsum(tallies), jnp.arange(rows * top), side="right").astype(jnp.int32)
    listing = items.reshape(top, rows).T
    listing = listing[jax.random.permutation(jax.random.fold_in(own, 1), rows)]
    offset_by = jax.random.randint(jax.random.fold_in(own, 2), (rows, 1), 0, top)
    return jnp.take_along_axis(listing, (jnp.arange(top)[None, :] + offset_by) % top, axis=1)


def load_shares(number_of, total, bound, lean, full):
    weights = [(1 << 20) // math.isqrt(grade ** lean) + 1 for grade in range(1, number_of + 1)]
    largest = bound if full else min(bound, max(-(-total // number_of), total * weights[0] // sum(weights)))
    least = 1 if total - largest >= number_of - 1 else 0
    counts, rest = [largest] + [least] * (number_of - 1), total - largest - least * (number_of - 1)
    while rest > 0:
        free = [i for i in range(1, number_of) if counts[i] < largest] or [i for i in range(1, number_of) if counts[i] < bound]
        whole, left = sum([weights[i] for i in free]), rest
        for i in free:
            more = min(bound - counts[i], max(1, left * weights[i] // whole), rest)
            counts[i] = counts[i] + more
            rest = rest - more
    return np.array(counts)


def gaussian(own_key, shape, deviation, limit, split=(), held_as=jnp.bfloat16):
    gain = shard_levels(own_key, shape, split, -0.22, 0.18) if split else 1.0
    entries = jax.random.normal(own_key, shape, jnp.float32) * deviation * gain
    return jnp.minimum(jnp.maximum(entries, -limit), limit).astype(held_as)


def setup_inputs(seed: int = 0, part: int = 0) -> dict:
    splits = jax.random.split(jax.random.key(seed), 9)
    part_keys = jax.random.split(jax.random.fold_in(splits[8], part), 9)
    parent_tiles = gaussian(part_keys[0], (PTILES, TILE, TILE), 1.0, 6.0, ((0, 32),), jnp.float32)
    parent_mean = gaussian(part_keys[1], (PTILES, TILE), 1.0, 6.0, ((0, 32),), jnp.float32)
    factor_w = gaussian(part_keys[2], (CHILDREN, KP * TILE, BJ), (KP * TILE) ** -0.5, 0.1875, ((0, 32),), jnp.float32)
    diag_inverse = gaussian(part_keys[3], (CHILDREN, BJ, BJ), 1.0, 6.0, ((0, 32),), jnp.float32)
    own_mean = gaussian(part_keys[4], (CHILDREN, BJ), 1.0, 6.0, ((0, 32),), jnp.float32)
    config_weight = jnp.clip(jnp.exp(jax.random.uniform(part_keys[5], (1,), jnp.float32, math.log(0.2), math.log(2.0))), 0.2, 2.0)
    need_owner_keys = jax.random.split(jax.random.fold_in(splits[6], 1), ITEMS // NEED_DEV)
    need_owner_turns = jax.random.permutation(jax.random.fold_in(splits[6], 3), ITEMS // NEED_DEV)
    need_owner = jax.vmap(lambda own, number: routed_block(jax.random.fold_in(splits[6], 2), own, number, NEED_DEV, N_FRONT, 1, CAP, 2))(need_owner_keys, need_owner_turns).reshape((ITEMS, 1))
    need_local = place_ends(jax.random.randint(splits[7], (ITEMS,), 0, PT_DEV), jax.random.fold_in(splits[7], 1), 0, PT_DEV - 1).astype(jnp.int32)
    return dict(parent_tiles=parent_tiles, parent_mean=parent_mean, factor_w=factor_w, diag_inverse=diag_inverse, own_mean=own_mean, config_weight=config_weight, need_owner=need_owner, need_local=need_local)


highest_precision = lax.Precision.HIGHEST


def reference(parent_tiles, parent_mean, factor_w, diag_inverse, own_mean, config_weight, need_owner, need_local):
    slot_index = (need_owner[:, 0] * PT_DEV + need_local).astype(jnp.int32)
    per_child = KP * KP
    diagonal_items = (jnp.arange(KP, dtype=jnp.int32) * (KP + 1)).astype(jnp.int32)

    def one_child(child_index):
        child_slots = lax.dynamic_slice_in_dim(slot_index, child_index * per_child, per_child)
        item_tiles = jnp.take(parent_tiles, child_slots, axis=0).reshape(KP, KP, TILE, TILE)
        factor = factor_w[child_index]
        blocks = factor.reshape(KP, TILE, BJ)
        sigma_pj = -jnp.einsum("abij,bjk->aik", item_tiles, blocks, precision=highest_precision).reshape(KP * TILE, BJ)
        sigma_jj = diag_inverse[child_index] - jnp.dot(factor.T, sigma_pj, precision=highest_precision, preferred_element_type=jnp.float32)
        parent_piece = jnp.take(parent_mean, child_slots[diagonal_items], axis=0).reshape(KP * TILE)
        mean_value = own_mean[child_index] - jnp.dot(parent_piece, factor, precision=highest_precision, preferred_element_type=jnp.float32)
        return sigma_pj, sigma_jj, jnp.diagonal(sigma_jj), mean_value

    sigma_pj, sigma_jj, variance, mean_value = lax.map(one_child, jnp.arange(N_FRONT * CH_DEV, dtype=jnp.int32))
    weight = config_weight[0]
    return sigma_pj, sigma_jj, weight * variance, weight * mean_value
```

```python
import functools

import jax
import jax.numpy as jnp
from jax import lax
from jax.experimental import pallas as pl
from jax.experimental.pallas import tpu as pltpu
from jax.sharding import PartitionSpec as P

highest_precision = lax.Precision.HIGHEST
MESH = pl.DeviceIdType.MESH

LEVELS = 8
CHIPS = 16
STORED = 8
CHIP_TILES = 16
SLOTS = 256
LINKS = 3
WINDOWS = 26
POOL = CHIP_TILES + 2 * LINKS * WINDOWS
RING = 4
REACH = 5
NONE = -1.0e6


def split_bf16(value):
    high = value.astype(jnp.bfloat16)
    return high, (value - high.astype(jnp.float32)).astype(jnp.bfloat16)


def dot3(left_high, left_low, right_high, right_low):
    def dot(left, right):
        return jnp.dot(left, right, preferred_element_type=jnp.float32)

    return dot(left_high, right_high) + (dot(left_high, right_low) + dot(left_low, right_high))


def plan_kernel(slots_ref, out_ref, table_ref, pool_ref):
    shape = (CHIPS, SLOTS)
    row = lax.broadcasted_iota(jnp.int32, shape, 0)
    lane = lax.broadcasted_iota(jnp.int32, shape, 1)
    chip_y, chip_z = row >> 3, row & 7
    owner_y, owner_z, owner_core = lane >> 7, (lane >> 4) & 7, (lane >> 3) & 1
    slots = slots_ref[...]
    need = jnp.zeros(shape, jnp.float32)
    for item in range(slots.shape[1]):
        need = jnp.where(slots[:, item : item + 1] == lane, 1.0, need)

    def swapped(value):
        return jnp.concatenate([value[LEVELS:], value[:LEVELS]], axis=0)

    def turned(value, by):
        return jnp.concatenate(
            [pltpu.roll(value[:LEVELS], by, 0), pltpu.roll(value[LEVELS:], by, 0)], axis=0
        )

    def most(value):
        return jnp.max(value, axis=0, keepdims=True)

    other_need = swapped(need)
    level_need = jnp.maximum(need, other_need) > 0.0
    ahead = ((chip_z - owner_z) & 7).astype(jnp.float32)
    behind = ((owner_z - chip_z) & 7).astype(jnp.float32)
    on_owner_line = chip_y == owner_y
    one_lane = lax.broadcasted_iota(jnp.int32, (1, SLOTS), 1)
    even = (one_lane & 1) == 0
    best = jnp.full((1, SLOTS), 1.0e6, jnp.float32)
    up = jnp.zeros((1, SLOTS), jnp.float32)
    down = jnp.zeros((1, SLOTS), jnp.float32)
    for cut in range(LEVELS - 1 - REACH, REACH + 1):
        cut_up = most(jnp.where(level_need & (ahead <= cut), ahead, 0.0))
        cut_down = most(jnp.where(level_need & (behind <= LEVELS - 1 - cut), behind, 0.0))
        cost = (cut_up + cut_down) * 100.0 + jnp.abs(cut_up - cut_down) * 10.0
        cost = cost + jnp.where((cut_up > cut_down) == even, 1.0, 0.0)
        better = cost < best
        best = jnp.where(better, cost, best)
        up = jnp.where(better, cut_up, up)
        down = jnp.where(better, cut_down, down)
    own_count = jnp.sum(jnp.where(on_owner_line & (ahead > 0.0), need, 0.0), axis=0, keepdims=True)
    other_count = jnp.sum(jnp.where(on_owner_line, 0.0, need), axis=0, keepdims=True)
    crosses = jnp.where(other_count - own_count - 1.0 > 0.0, 1.0, 0.0)
    on_line = jnp.where(on_owner_line, 1.0 - crosses, crosses) > 0.0
    at_owner = on_owner_line & (ahead == 0.0)
    at_level = ahead == 0.0
    send_up = on_line & (ahead < up)
    send_down = on_line & (behind < down)
    reached = (ahead <= up) | (behind <= down)
    crossing = at_owner & (crosses > 0.0)
    send_over = crossing | (
        on_line & reached & (other_need > 0.0) & jnp.logical_not(at_level & (crosses > 0.0))
    )
    end_up = most(jnp.where(on_line & (ahead == up), other_need, 0.0))
    end_down = most(jnp.where(on_line & (behind == down), other_need, 0.0))
    longest = jnp.maximum(2.0 * up + end_up, 2.0 * down + end_down)
    rank_up = 2.0 * (up - ahead) + end_up
    rank_down = 2.0 * (down - behind) + end_down
    rank_over = jnp.where(crossing, longest + 2.0, 1.0)
    key_up = jnp.where(send_up, rank_up * 256.0, NONE)
    key_down = jnp.where(send_down, rank_down * 256.0, NONE)
    key_over = jnp.where(send_over, rank_over * 256.0, NONE)
    held = jnp.where(at_owner, (255 - (lane & 15)).astype(jnp.float32), NONE)

    def window(w, carry):
        keys, held, coming, table = list(carry[:3]), carry[3], carry[4], carry[5]
        arrives = []
        for link in range(LINKS):
            sent = jnp.full(shape, NONE, jnp.float32)
            for core in range(2):
                key = keys[link] + held
                key = jnp.where((owner_core == core) | (w >= 2), key, NONE)
                top = jnp.max(key, axis=1, keepdims=True)
                hit = (key == top) & (top > 0.0)
                keys[link] = jnp.where(hit, NONE, keys[link])
                place = CHIP_TILES + link * 2 * WINDOWS + 2 * w + core
                sent = jnp.where(hit, (255 - place).astype(jnp.float32), sent)
                found = jnp.where(top > 0.0, 255 - (top.astype(jnp.int32) & 255), 0)
                table = jnp.where(lane == 6 * w + 2 * link + core, found, table)
            arrives.append(sent)
        fresh = jnp.maximum(
            jnp.maximum(turned(arrives[0], 1), turned(arrives[1], LEVELS - 1)), swapped(arrives[2])
        )
        return (*keys, jnp.maximum(held, coming), fresh, table)

    carry = (
        key_up,
        key_down,
        key_over,
        held,
        jnp.full(shape, NONE, jnp.float32),
        jnp.zeros(shape, jnp.int32),
    )
    key_up, key_down, key_over, held, coming, table = lax.fori_loop(0, WINDOWS, window, carry)
    held = jnp.maximum(held, coming)
    table_ref[...] = table
    pool_ref[...] = jnp.where(held >= 0.0, 255 - held.astype(jnp.int32), 0)
    left = jnp.maximum(jnp.maximum(key_up, key_down), key_over)
    fits = jnp.where(jnp.max(left) > 0.0, 0, 1)
    chip = lax.axis_index("front") // 2
    out_ref[...] = jnp.zeros(out_ref.shape, jnp.int32)
    out_ref[0:1, :] = table_ref[pl.ds(chip, 1), :]
    out_ref[1:2, :] = pool_ref[pl.ds(chip, 1), :]
    out_ref[2:3, :] = jnp.full((1, SLOTS), fits, jnp.int32)


def exchange_kernel(
    plan_ref,
    item_ref,
    weight_ref,
    tiles_ref,
    mean_ref,
    factor_ref,
    diag_ref,
    own_mean_ref,
    pj_ref,
    jj_ref,
    variance_ref,
    out_mean_ref,
    pool,
    land,
    passed,
    outgoing,
    high,
    low,
    turned_high,
    turned_low,
    stage,
    jj,
    means,
    send_sem,
    land_sem,
    pass_send_sem,
    pass_sem,
    swap_sem,
    ring_send_sem,
    ring_sem,
    mean_sem,
    stage_sem,
    jj_sem,
    out_sem,
    credit,
    pass_credit,
):
    cfg, me = lax.axis_index("cfg"), lax.axis_index("front")
    y, z, core = me // 16, (me // 2) % 8, me % 2
    children = factor_ref.shape[0]

    def device(to_y, to_z, to_core):
        return (cfg, to_y * 16 + to_z * 2 + to_core)

    above = device(y, (z + 1) % 8, core)
    below = device(y, (z + 7) % 8, core)
    across = device(1 - y, z, core)
    partner = device(y, z, 1 - core)
    targets = (above, below, across)
    sources = (below, above, across)

    def signal(sem, to):
        pl.semaphore_signal(sem, inc=1, device_id=to, device_id_type=MESH)

    def remote(src, dst, sent, got, to):
        return pltpu.make_async_remote_copy(
            src_ref=src,
            dst_ref=dst,
            send_sem=sent,
            recv_sem=got,
            device_id=to,
            device_id_type=MESH,
        )

    def load_stage(child):
        return pltpu.make_async_copy(factor_ref.at[child], stage, stage_sem)

    jj_load = pltpu.make_async_copy(diag_ref, jj, jj_sem.at[0])
    load_stage(0).start()
    jj_load.start()
    barrier = pltpu.get_barrier_semaphore()
    for neighbour in (above, below, across, partner):
        signal(barrier, neighbour)
    line = y * 2 + core
    means[line, z] = mean_ref[...]
    pl.semaphore_wait(barrier, 4)

    own = pl.ds(core * STORED, STORED)
    swap = remote(tiles_ref, pool.at[own], swap_sem.at[0], swap_sem.at[1], partner)

    def ring(step):
        block = means.at[line, (z + 8 - step) % 8]
        return remote(block, block, ring_send_sem.at[step], ring_sem.at[step], above)

    def send(w, link):
        return remote(
            outgoing.at[link, w % 2],
            land.at[link * RING + w % RING],
            send_sem.at[link, w % 2],
            land_sem.at[link, w % RING],
            targets[link],
        )

    def hand_over(v, link):
        place = link * RING + v % RING
        return remote(
            land.at[place],
            passed.at[place],
            pass_send_sem.at[link, v % RING],
            pass_sem.at[link, v % RING],
            partner,
        )

    for w in range(2):
        for link in range(LINKS):
            outgoing[link, w] = tiles_ref[plan_ref[0, 6 * w + 2 * link + core] % STORED]
            send(w, link).start()
        if w == 0:
            swap.start()
            ring(0).start()

    def keep(tile, carry):
        pool[core * STORED + tile] = tiles_ref[tile]
        return carry

    lax.fori_loop(0, STORED, keep, 0)
    swap.wait()

    def take(v):
        for link in range(LINKS):
            send(v, link).wait_recv()

            @pl.when(v >= RING)
            def _():
                pl.semaphore_wait(pass_credit.at[link], 1)

            hand_over(v, link).start()
        for link in range(LINKS):
            place = CHIP_TILES + link * 2 * WINDOWS + 2 * v
            pool[place + core] = land[link * RING + v % RING]
        for link in range(LINKS):
            hand_over(v, link).wait_send()

            @pl.when(v < WINDOWS - RING)
            def _():
                signal(credit.at[link], sources[link])

        for link in range(LINKS):
            hand_over(v, link).wait_recv()
            place = CHIP_TILES + link * 2 * WINDOWS + 2 * v
            pool[place + 1 - core] = passed[link * RING + v % RING]

            @pl.when(v < WINDOWS - RING)
            def _():
                signal(pass_credit.at[link], partner)

    both = means.at[pl.ds(y * 2, 2)]
    line_swap = remote(means.at[line], means.at[line], mean_sem.at[0], mean_sem.at[1], partner)
    mean_swap = remote(both, both, mean_sem.at[2], mean_sem.at[3], across)

    def window(w, carry):
        take(w - 2)
        for link in range(LINKS):
            send(w, link).wait_send()
            outgoing[link, w % 2] = pool[plan_ref[0, 6 * w + 2 * link + core]]

            @pl.when(w >= RING)
            def _():
                pl.semaphore_wait(credit.at[link], 1)

            send(w, link).start()

        @pl.when(w < 9)
        def _():
            ring(w - 2).wait()

            @pl.when(w < 8)
            def _():
                ring(w - 1).start()

        @pl.when(w == 9)
        def _():
            line_swap.start()

        @pl.when(w == 10)
        def _():
            line_swap.wait()
            mean_swap.start()

        @pl.when(w == 11)
        def _():
            mean_swap.wait()

        @pl.when((w >= 3) & (w < 3 + children))
        def _():
            child = w - 3
            load_stage(child).wait()
            for b in range(4):
                rows = pl.ds(child * 1024 + b * 256, 256)
                block = stage[b * 256 : (b + 1) * 256, :]
                high[rows, :], low[rows, :] = split_bf16(block)
                cols = pl.ds(b * 256, 256)
                block_t = block.T
                turned_high[child, :, cols], turned_low[child, :, cols] = split_bf16(block_t)

            @pl.when(child + 1 < children)
            def _():
                load_stage(child + 1).start()

        return carry

    lax.fori_loop(2, WINDOWS, window, 0)
    take(WINDOWS - 2)
    take(WINDOWS - 1)
    for w in range(WINDOWS - 2, WINDOWS):
        for link in range(LINKS):
            send(w, link).wait_send()
    jj_load.wait()

    weight = weight_ref[0]
    rows_at = lax.broadcasted_iota(jnp.int32, (256, 256), 0)
    cols_at = lax.broadcasted_iota(jnp.int32, (256, 256), 1)

    def pj_out(place):
        return pltpu.make_async_copy(
            land.at[place], pj_ref.at[place // 4, pl.ds((place % 4) * 256, 256)], out_sem.at[place]
        )

    def jj_out(child):
        return pltpu.make_async_copy(jj.at[child], jj_ref.at[child], jj_sem.at[child])

    def front(child, carry):
        def pattern_row(a, carry):
            total = jnp.zeros((256, 256), jnp.float32)
            for b in range(4):
                item = plan_ref[1, item_ref[child * 16 + a * 4 + b]]
                tile_high, tile_low = split_bf16(pool[item])
                rows = pl.ds(child * 1024 + b * 256, 256)
                total += dot3(tile_high, tile_low, high[rows, :], low[rows, :])
            block = -total
            place = child * 4 + a
            land[place] = block
            pj_out(place).start()
            block_high, block_low = split_bf16(block)
            cols = pl.ds(pl.multiple_of(a * 256, 256), 256)
            jj[child] -= dot3(
                turned_high[child, :, cols], turned_low[child, :, cols], block_high, block_low
            )
            return carry

        lax.fori_loop(0, 4, pattern_row, 0)
        jj_out(child).start()
        diagonal = jnp.where(rows_at == cols_at, jj[child], 0.0)
        variance_ref[pl.ds(child, 1), :] = weight * jnp.sum(diagonal, axis=0, keepdims=True)
        total = jnp.zeros((16, 256), jnp.float32)
        for a in range(4):
            slot = item_ref[child * 16 + a * 5]
            slot_line = slot // 128 * 2 + slot // 8 % 2
            piece = means[slot_line, slot // 16 % 8, pl.ds(slot % 8, 1), :]
            piece_high, piece_low = split_bf16(jnp.broadcast_to(piece, (16, 256)))
            rows = pl.ds(child * 1024 + a * 256, 256)
            total += dot3(piece_high, piece_low, high[rows, :], low[rows, :])
        value = own_mean_ref[pl.ds(child, 1), :] - total[0:1]
        out_mean_ref[pl.ds(child, 1), :] = weight * value
        return carry

    lax.fori_loop(0, children, front, 0)
    for child in range(children):
        for a in range(4):
            pj_out(child * 4 + a).wait()
        jj_out(child).wait()


def exchange(plan, items, parent_tiles, parent_mean, factor_w, diag_inverse, own_mean, config_weight):
    tile = parent_tiles.shape[1:]
    children, depth, width = factor_w.shape
    vmem = pl.BlockSpec(memory_space=pltpu.VMEM)
    smem = pl.BlockSpec(memory_space=pltpu.SMEM)
    anywhere = pl.BlockSpec(memory_space=pl.ANY)
    dma = pltpu.SemaphoreType.DMA
    f32, bf16 = jnp.float32, jnp.bfloat16
    return pl.pallas_call(
        exchange_kernel,
        out_shape=(
            jax.ShapeDtypeStruct(factor_w.shape, f32),
            jax.ShapeDtypeStruct(diag_inverse.shape, f32),
            jax.ShapeDtypeStruct(own_mean.shape, f32),
            jax.ShapeDtypeStruct(own_mean.shape, f32),
        ),
        in_specs=[smem, smem, smem, vmem, vmem, anywhere, anywhere, vmem],
        out_specs=(anywhere, anywhere, vmem, vmem),
        scratch_shapes=[
            pltpu.VMEM((POOL, *tile), f32),
            pltpu.VMEM((LINKS * RING, *tile), f32),
            pltpu.VMEM((LINKS * RING, *tile), f32),
            pltpu.VMEM((LINKS, 2, *tile), f32),
            pltpu.VMEM((children * depth, width), bf16),
            pltpu.VMEM((children * depth, width), bf16),
            pltpu.VMEM((children, width, depth), bf16),
            pltpu.VMEM((children, width, depth), bf16),
            pltpu.VMEM((depth, width), f32),
            pltpu.VMEM(diag_inverse.shape, f32),
            pltpu.VMEM((4, LEVELS, *parent_mean.shape), f32),
            dma((LINKS, 2)),
            dma((LINKS, RING)),
            dma((LINKS, RING)),
            dma((LINKS, RING)),
            dma((2,)),
            dma((LEVELS - 1,)),
            dma((LEVELS - 1,)),
            dma((4,)),
            dma,
            dma((children,)),
            dma((LINKS * RING,)),
            pltpu.SemaphoreType.REGULAR((LINKS,)),
            pltpu.SemaphoreType.REGULAR((LINKS,)),
        ],
        compiler_params=pltpu.CompilerParams(
            collective_id=0, has_side_effects=True, vmem_limit_bytes=63 << 20
        ),
    )(plan, items, config_weight, parent_tiles, parent_mean, factor_w, diag_inverse, own_mean)


def any_reads(
    parent_tiles,
    parent_mean,
    factor_w,
    diag_inverse,
    own_mean,
    config_weight,
    need_owner,
    need_local,
):
    fronts = lax.axis_size("front")
    myself = lax.axis_index("front")
    stored = parent_tiles.shape[0]
    tile_size = parent_tiles.shape[1]
    child_count = factor_w.shape[0]
    own_cols = factor_w.shape[2]
    pattern = factor_w.shape[1] // tile_size
    need_count = child_count * pattern * pattern
    capacity = max(2, need_count // fronts + 1)
    owner_table = need_owner[:, 0].reshape(fronts, need_count)
    local_table = need_local.reshape(fronts, need_count)
    positions = jnp.arange(need_count, dtype=jnp.int32)
    earlier = positions[None, :] < positions[:, None]
    same_owner = owner_table[:, :, None] == owner_table[:, None, :]
    item_rank = jnp.sum(same_owner & earlier[None], axis=2)
    slot_range = jnp.arange(capacity, dtype=jnp.int32)
    outgoing = (owner_table[:, None, :] == myself) & (
        item_rank[:, None, :] == slot_range[None, :, None]
    )
    send_local = jnp.sum(jnp.where(outgoing, local_table[:, None, :], 0), axis=2).reshape(-1)
    send_mask = jnp.any(outgoing, axis=2).reshape(-1).astype(jnp.float32)
    my_owner = lax.dynamic_index_in_dim(owner_table, myself, 0, keepdims=False)
    my_rank = lax.dynamic_index_in_dim(item_rank, myself, 0, keepdims=False)
    my_local = lax.dynamic_index_in_dim(local_table, myself, 0, keepdims=False)
    arrival = my_owner * capacity + my_rank
    pair_index = jnp.arange(child_count * pattern, dtype=jnp.int32)
    diagonal_items = pair_index // pattern * pattern * pattern + pair_index % pattern * (
        pattern + 1
    )
    tile_buffer = (jnp.take(parent_tiles, send_local, axis=0) * send_mask[:, None, None]).reshape(
        fronts, capacity, tile_size, tile_size
    )
    received = lax.all_to_all(tile_buffer, "front", split_axis=0, concat_axis=0, tiled=True)
    item_tiles = jnp.take(
        received.reshape(fronts * capacity, tile_size, tile_size), arrival, axis=0
    )
    item_tiles = item_tiles.reshape(child_count, pattern, pattern, tile_size, tile_size)
    blocks = factor_w.reshape(child_count, pattern, tile_size, own_cols)
    sigma_pj = -jnp.einsum("cabij,cbjk->caik", item_tiles, blocks, precision=highest_precision)
    sigma_pj = sigma_pj.reshape(child_count, pattern * tile_size, own_cols)
    full_mean = lax.all_gather(parent_mean, "front", axis=0, tiled=True)
    parent_piece = jnp.take(full_mean, (my_owner * stored + my_local)[diagonal_items], axis=0)
    parent_piece = parent_piece.reshape(child_count, pattern * tile_size)
    sigma_jj = diag_inverse - jnp.einsum(
        "cpj,cpk->cjk", factor_w, sigma_pj, precision=highest_precision
    )
    variance = jnp.diagonal(sigma_jj, axis1=1, axis2=2)
    mean_value = own_mean - jnp.einsum(
        "cp,cpj->cj", parent_piece, factor_w, precision=highest_precision
    )
    weight = config_weight[0]
    return (sigma_pj, sigma_jj, weight * variance, weight * mean_value)


def shards(
    parent_tiles,
    parent_mean,
    factor_w,
    diag_inverse,
    own_mean,
    config_weight,
    need_owner,
    need_local,
):
    slots = need_owner[:, 0] * STORED + need_local
    plan = pl.pallas_call(
        plan_kernel,
        out_shape=jax.ShapeDtypeStruct((8, SLOTS), jnp.int32),
        in_specs=[pl.BlockSpec(memory_space=pltpu.VMEM)],
        out_specs=pl.BlockSpec(memory_space=pltpu.VMEM),
        scratch_shapes=[pltpu.VMEM((CHIPS, SLOTS), jnp.int32)] * 2,
    )(slots.reshape(CHIPS, -1))
    items = slots.shape[0] // lax.axis_size("front")
    mine = lax.dynamic_slice_in_dim(slots, lax.axis_index("front") * items, items)
    operands = (parent_tiles, parent_mean, factor_w, diag_inverse, own_mean, config_weight)
    return lax.cond(
        plan[2, 0] > 0,
        lambda: exchange(plan, mine, *operands),
        lambda: any_reads(*operands, need_owner, need_local),
    )


def solution(mesh):
    return jax.shard_map(
        shards,
        mesh=mesh,
        in_specs=(
            P(("cfg", "front"), None, None),
            P(("cfg", "front"), None),
            P(("cfg", "front"), None, None),
            P(("cfg", "front"), None, None),
            P(("cfg", "front"), None),
            P("cfg"),
            P(),
            P(),
        ),
        out_specs=(
            P(("cfg", "front"), None, None),
            P(("cfg", "front"), None, None),
            P(("cfg", "front"), None),
            P(("cfg", "front"), None),
        ),
        check_vma=False,
    )
```

```python
import functools

import jax
import jax.numpy as jnp
from jax import lax
from jax.experimental import pallas as pl
from jax.experimental.pallas import tpu as pltpu
from jax.sharding import PartitionSpec as P

highest_precision = lax.Precision.HIGHEST
MESH = pl.DeviceIdType.MESH

LEVELS = 8
CHIPS = 16
STORED = 8
CHIP_TILES = 16
SLOTS = 256
LINKS = 3
WINDOWS = 23
POOL = CHIP_TILES + 2 * LINKS * WINDOWS
RING = 4
REACH = 5
NONE = -1.0e6
ROUNDS = 2
STEEP = 0.03


def split_bf16(value):
    high = value.astype(jnp.bfloat16)
    return high, (value - high.astype(jnp.float32)).astype(jnp.bfloat16)


def dot3(left_high, left_low, right_high, right_low):
    def dot(left, right):
        return jnp.dot(left, right, preferred_element_type=jnp.float32)

    return dot(left_high, right_high) + (dot(left_high, right_low) + dot(left_low, right_high))


def swapped(value):
    return jnp.concatenate([value[LEVELS:], value[:LEVELS]], axis=0)


def turned(value, by):
    return jnp.concatenate(
        [pltpu.roll(value[:LEVELS], by, 0), pltpu.roll(value[LEVELS:], by, 0)], axis=0
    )


def most(value):
    return jnp.max(value, axis=0, keepdims=True)


def choose_routes(slots, uses_ref):
    shape = (CHIPS, SLOTS)
    row = lax.broadcasted_iota(jnp.int32, shape, 0)
    lane = lax.broadcasted_iota(jnp.int32, shape, 1)
    one_lane = lax.broadcasted_iota(jnp.int32, (1, SLOTS), 1)
    chip_y, chip_z = row >> 3, row & 7
    owner_y, owner_z = lane >> 7, (lane >> 4) & 7
    need = jnp.zeros(shape, jnp.float32)
    for item in range(slots.shape[1]):
        need = jnp.where(slots[:, item : item + 1] == lane, 1.0, need)
    other_need = swapped(need)
    level_need = jnp.maximum(need, other_need) > 0.0
    ahead = ((chip_z - owner_z) & 7).astype(jnp.float32)
    behind = ((owner_z - chip_z) & 7).astype(jnp.float32)
    own_line = jnp.where(chip_y == owner_y, 1.0, 0.0)
    at_level = jnp.where(ahead == 0.0, 1.0, 0.0)
    at_owner = own_line * at_level
    ups, downs = [], []
    for option, cut in enumerate(range(LEVELS - 1 - REACH, REACH + 1)):
        up = most(jnp.where(level_need & (ahead <= cut), ahead, 0.0))
        down = most(jnp.where(level_need & (behind <= LEVELS - 1 - cut), behind, 0.0))
        ups.append(up)
        downs.append(down)
        uses_ref[option, 0] = jnp.where(ahead < up, 1.0, 0.0)
        uses_ref[option, 1] = jnp.where(behind < down, 1.0, 0.0)
        reached = jnp.where((ahead <= up) | (behind <= down), other_need, 0.0)
        uses_ref[option, 2] = reached * (1.0 - at_level * (1.0 - own_line))

    def sends(up, down, crosses):
        on_line = own_line * (1.0 - crosses) + (1.0 - own_line) * crosses
        reached = jnp.where((ahead <= up) | (behind <= down), on_line * other_need, 0.0)
        return (
            jnp.where(ahead < up, on_line, 0.0),
            jnp.where(behind < down, on_line, 0.0),
            reached * (1.0 - at_level * crosses) + at_owner * crosses,
            on_line,
        )

    def settle(step, carry):
        choice, up, down, crosses = carry
        steep = jnp.where(step == 0, 0.0, STEEP)
        weights = [
            jnp.exp(steep * (jnp.sum(use, axis=1, keepdims=True) - 40.0))
            for use in sends(up, down, crosses)[:3]
        ]
        over = jnp.sum(at_owner * weights[2], axis=0, keepdims=True)
        best = jnp.full((1, SLOTS), 1.0e9, jnp.float32)
        chosen = [jnp.zeros((1, SLOTS), jnp.float32)] * 4
        for option in range(len(ups)):
            cost = sum(uses_ref[option, link] * weights[link] for link in range(LINKS))
            first = jnp.sum(cost[:LEVELS], axis=0, keepdims=True)
            second = jnp.sum(cost[LEVELS:], axis=0, keepdims=True)
            for side in range(2):
                total = jnp.where((one_lane < SLOTS // 2) == (side == 0), first, second)
                total = total + over * float(side)
                number = 2.0 * option + side
                total = jnp.where(choice == number, total - 0.1, total)
                better = total < best
                best = jnp.where(better, total, best)
                values = (number, ups[option], downs[option], float(side))
                chosen = [jnp.where(better, v, c) for v, c in zip(values, chosen)]
        turn = ((one_lane & 15) == ((step - 1) & 15)) | (step == 0)
        return tuple(jnp.where(turn, c, old) for c, old in zip(chosen, carry))

    start = (jnp.full((1, SLOTS), -1.0, jnp.float32),) + (jnp.zeros((1, SLOTS), jnp.float32),) * 3
    choice, up, down, crosses = lax.fori_loop(0, 1 + 16 * ROUNDS, settle, start)
    send_up, send_down, send_over, on_line = sends(up, down, crosses)
    end_up = most(jnp.where(ahead == up, on_line * other_need, 0.0))
    end_down = most(jnp.where(behind == down, on_line * other_need, 0.0))
    longest = jnp.maximum(2.0 * up + 3.0 * end_up, 2.0 * down + 3.0 * end_down)
    rank_up = 2.0 * (up - ahead) + 3.0 * end_up + 2.0 * turned(other_need, LEVELS - 1)
    rank_down = 2.0 * (down - behind) + 3.0 * end_down + 2.0 * turned(other_need, 1)
    rank_over = jnp.where(at_owner * crosses > 0.0, longest + 2.0, 1.0)
    return (
        jnp.where(send_up > 0.0, rank_up * 256.0, NONE),
        jnp.where(send_down > 0.0, rank_down * 256.0, NONE),
        jnp.where(send_over > 0.0, rank_over * 256.0, NONE),
        jnp.where(at_owner > 0.0, (255 - (lane & 15)).astype(jnp.float32), NONE),
        jnp.full(shape, NONE, jnp.float32),
        jnp.zeros(shape, jnp.int32),
    )


def schedule(w, carry):
    keys, held, coming, table = list(carry[:3]), carry[3], carry[4], carry[5]
    shape = held.shape
    lane = lax.broadcasted_iota(jnp.int32, shape, 1)
    arrives = []
    for link in range(LINKS):
        sent = jnp.full(shape, NONE, jnp.float32)
        for core in range(2):
            key = keys[link] + held
            key = jnp.where((((lane >> 3) & 1) == core) | (w >= 2), key, NONE)
            top = jnp.max(key, axis=1, keepdims=True)
            hit = (key == top) & (top > 0.0)
            keys[link] = jnp.where(hit, NONE, keys[link])
            place = CHIP_TILES + link * 2 * WINDOWS + 2 * w + core
            sent = jnp.where(hit, jnp.asarray(255 - place).astype(jnp.float32), sent)
            found = jnp.where(top > 0.0, 255 - (top.astype(jnp.int32) & 255), 0)
            table = jnp.where(lane == 6 * w + 2 * link + core, found, table)
        arrives.append(sent)
    fresh = jnp.maximum(
        jnp.maximum(turned(arrives[0], 1), turned(arrives[1], LEVELS - 1)), swapped(arrives[2])
    )
    return (*keys, jnp.maximum(held, coming), fresh, table)


def exchange_kernel(
    owner_ref,
    local_ref,
    owner_item_ref,
    local_item_ref,
    weight_ref,
    tiles_ref,
    mean_ref,
    factor_ref,
    diag_ref,
    own_mean_ref,
    pj_ref,
    jj_ref,
    variance_ref,
    out_mean_ref,
    fits_ref,
    pool,
    land,
    passed,
    outgoing,
    high,
    low,
    turned_high,
    turned_low,
    stage,
    jj,
    means,
    uses,
    whole,
    rows_out,
    first_plan,
    plan,
    send_sem,
    land_sem,
    pass_send_sem,
    pass_sem,
    swap_sem,
    ring_send_sem,
    ring_sem,
    mean_sem,
    stage_sem,
    jj_sem,
    out_sem,
    plan_sem,
    credit,
    pass_credit,
):
    cfg, me = lax.axis_index("cfg"), lax.axis_index("front")
    y, z, core = me // 16, (me // 2) % 8, me % 2
    children = factor_ref.shape[0]

    def device(to_y, to_z, to_core):
        return (cfg, to_y * 16 + to_z * 2 + to_core)

    above = device(y, (z + 1) % 8, core)
    below = device(y, (z + 7) % 8, core)
    across = device(1 - y, z, core)
    partner = device(y, z, 1 - core)
    targets = (above, below, across)
    sources = (below, above, across)

    def signal(sem, to):
        pl.semaphore_signal(sem, inc=1, device_id=to, device_id_type=MESH)

    def remote(src, dst, sent, got, to):
        return pltpu.make_async_remote_copy(
            src_ref=src,
            dst_ref=dst,
            send_sem=sent,
            recv_sem=got,
            device_id=to,
            device_id_type=MESH,
        )

    def load_stage(child):
        return pltpu.make_async_copy(factor_ref.at[child], stage, stage_sem)

    jj_load = pltpu.make_async_copy(diag_ref, jj, jj_sem.at[0])
    load_stage(0).start()
    jj_load.start()
    barrier = pltpu.get_barrier_semaphore()
    for neighbour in (above, below, across, partner):
        signal(barrier, neighbour)
    line = y * 2 + core
    means[line, z] = mean_ref[...]
    routes = choose_routes(owner_ref[...] * STORED + local_ref[...], uses)
    routes = lax.fori_loop(0, 2, schedule, routes)

    def own_row(at, values):
        whole[...] = values
        rows_out[at : at + 1, :] = whole[pl.ds(me // 2, 1), :]

    own_row(0, routes[5])
    first_copy = pltpu.make_async_copy(rows_out, first_plan, plan_sem)
    first_copy.start()
    first_copy.wait()
    pl.semaphore_wait(barrier, 4)

    own = pl.ds(core * STORED, STORED)
    swap = remote(tiles_ref, pool.at[own], swap_sem.at[0], swap_sem.at[1], partner)

    def ring(step):
        block = means.at[line, (z + 8 - step) % 8]
        return remote(block, block, ring_send_sem.at[step], ring_sem.at[step], above)

    def send(w, link):
        return remote(
            outgoing.at[link, w % 2],
            land.at[link * RING + w % RING],
            send_sem.at[link, w % 2],
            land_sem.at[link, w % RING],
            targets[link],
        )

    def hand_over(v, link):
        place = link * RING + v % RING
        return remote(
            land.at[place],
            passed.at[place],
            pass_send_sem.at[link, v % RING],
            pass_sem.at[link, v % RING],
            partner,
        )

    def planned(table, w, link):
        return jnp.clip(table[0, 6 * w + 2 * link + core], 0, POOL - 1)

    for w in range(2):
        for link in range(LINKS):
            outgoing[link, w] = tiles_ref[planned(first_plan, w, link) % STORED]
            send(w, link).start()
        if w == 0:
            swap.start()
            ring(0).start()

    def keep(tile, carry):
        pool[core * STORED + tile] = tiles_ref[tile]
        return carry

    lax.fori_loop(0, STORED, keep, 0)
    key_up, key_down, key_over, held, coming, table = lax.fori_loop(2, WINDOWS, schedule, routes)
    held = jnp.maximum(held, coming)
    own_row(0, table)
    own_row(1, jnp.where(held >= 0.0, 255 - held.astype(jnp.int32), 0))
    plan_copy = pltpu.make_async_copy(rows_out, plan, plan_sem)
    plan_copy.start()
    left = jnp.maximum(jnp.maximum(key_up, key_down), key_over)
    fits_ref[0] = jnp.where(jnp.max(left) > 0.0, 0, 1)
    plan_copy.wait()
    swap.wait()

    def take(v):
        for link in range(LINKS):
            send(v, link).wait_recv()

            @pl.when(v >= RING)
            def _():
                pl.semaphore_wait(pass_credit.at[link], 1)

            hand_over(v, link).start()
        for link in range(LINKS):
            place = CHIP_TILES + link * 2 * WINDOWS + 2 * v
            pool[place + core] = land[link * RING + v % RING]
        for link in range(LINKS):
            hand_over(v, link).wait_send()

            @pl.when(v < WINDOWS - RING)
            def _():
                signal(credit.at[link], sources[link])

        for link in range(LINKS):
            hand_over(v, link).wait_recv()
            place = CHIP_TILES + link * 2 * WINDOWS + 2 * v
            pool[place + 1 - core] = passed[link * RING + v % RING]

            @pl.when(v < WINDOWS - RING)
            def _():
                signal(pass_credit.at[link], partner)

    both = means.at[pl.ds(y * 2, 2)]
    line_swap = remote(means.at[line], means.at[line], mean_sem.at[0], mean_sem.at[1], partner)
    mean_swap = remote(both, both, mean_sem.at[2], mean_sem.at[3], across)

    def slot_of(item):
        at = core * (children * 16) + item
        return owner_item_ref[me // 2, at] * STORED + local_item_ref[me // 2, at]

    weight = weight_ref[0]

    def weigh_mean(child):
        total = jnp.zeros((16, 256), jnp.float32)
        for a in range(4):
            slot = slot_of(child * 16 + a * 5)
            slot_line = slot // 128 * 2 + slot // 8 % 2
            piece = means[slot_line, slot // 16 % 8, pl.ds(slot % 8, 1), :]
            piece_high, piece_low = split_bf16(jnp.broadcast_to(piece, (16, 256)))
            rows = pl.ds(child * 1024 + a * 256, 256)
            total += dot3(piece_high, piece_low, high[rows, :], low[rows, :])
        value = own_mean_ref[pl.ds(child, 1), :] - total[0:1]
        out_mean_ref[pl.ds(child, 1), :] = weight * value

    def window(w, carry):
        take(w - 2)
        for link in range(LINKS):
            send(w, link).wait_send()
            outgoing[link, w % 2] = pool[planned(plan, w, link)]

            @pl.when(w >= RING)
            def _():
                pl.semaphore_wait(credit.at[link], 1)

            send(w, link).start()

        @pl.when(w < 9)
        def _():
            ring(w - 2).wait()

            @pl.when(w < 8)
            def _():
                ring(w - 1).start()

        @pl.when(w == 9)
        def _():
            line_swap.start()

        @pl.when(w == 10)
        def _():
            line_swap.wait()
            mean_swap.start()

        @pl.when(w == 11)
        def _():
            mean_swap.wait()

        @pl.when((w >= 12) & (w < 12 + children))
        def _():
            weigh_mean(w - 12)

        @pl.when((w >= 3) & (w < 3 + children))
        def _():
            child = w - 3
            load_stage(child).wait()
            for b in range(4):
                rows = pl.ds(child * 1024 + b * 256, 256)
                block = stage[b * 256 : (b + 1) * 256, :]
                high[rows, :], low[rows, :] = split_bf16(block)
                cols = pl.ds(b * 256, 256)
                block_t = block.T
                turned_high[child, :, cols], turned_low[child, :, cols] = split_bf16(block_t)

            @pl.when(child + 1 < children)
            def _():
                load_stage(child + 1).start()

        return carry

    lax.fori_loop(2, WINDOWS, window, 0)
    take(WINDOWS - 2)
    take(WINDOWS - 1)
    for w in range(WINDOWS - 2, WINDOWS):
        for link in range(LINKS):
            send(w, link).wait_send()
    jj_load.wait()

    rows_at = lax.broadcasted_iota(jnp.int32, (256, 256), 0)
    cols_at = lax.broadcasted_iota(jnp.int32, (256, 256), 1)

    def pj_out(place):
        return pltpu.make_async_copy(
            land.at[place], pj_ref.at[place // 4, pl.ds((place % 4) * 256, 256)], out_sem.at[place]
        )

    def jj_out(child):
        return pltpu.make_async_copy(jj.at[child], jj_ref.at[child], jj_sem.at[child])

    def front(child, carry):
        def pattern_row(a, carry):
            total = jnp.zeros((256, 256), jnp.float32)
            for b in range(4):
                item = jnp.clip(plan[1, slot_of(child * 16 + a * 4 + b)], 0, POOL - 1)
                tile_high, tile_low = split_bf16(pool[item])
                rows = pl.ds(child * 1024 + b * 256, 256)
                total += dot3(tile_high, tile_low, high[rows, :], low[rows, :])
            block = -total
            place = child * 4 + a
            land[place] = block
            pj_out(place).start()
            block_high, block_low = split_bf16(block)
            cols = pl.ds(pl.multiple_of(a * 256, 256), 256)
            jj[child] -= dot3(
                turned_high[child, :, cols], turned_low[child, :, cols], block_high, block_low
            )
            return carry

        lax.fori_loop(0, 4, pattern_row, 0)
        jj_out(child).start()
        diagonal = jnp.where(rows_at == cols_at, jj[child], 0.0)
        variance_ref[pl.ds(child, 1), :] = weight * jnp.sum(diagonal, axis=0, keepdims=True)
        return carry

    lax.fori_loop(0, children, front, 0)
    for child in range(children):
        for a in range(4):
            pj_out(child * 4 + a).wait()
        jj_out(child).wait()


def exchange(owners, locals_, parent_tiles, parent_mean, factor_w, diag_inverse, own_mean, config_weight):
    tile = parent_tiles.shape[1:]
    children, depth, width = factor_w.shape
    vmem = pl.BlockSpec(memory_space=pltpu.VMEM)
    smem = pl.BlockSpec(memory_space=pltpu.SMEM)
    anywhere = pl.BlockSpec(memory_space=pl.ANY)
    dma = pltpu.SemaphoreType.DMA
    f32, bf16 = jnp.float32, jnp.bfloat16
    return pl.pallas_call(
        exchange_kernel,
        out_shape=(
            jax.ShapeDtypeStruct(factor_w.shape, f32),
            jax.ShapeDtypeStruct(diag_inverse.shape, f32),
            jax.ShapeDtypeStruct(own_mean.shape, f32),
            jax.ShapeDtypeStruct(own_mean.shape, f32),
            jax.ShapeDtypeStruct((1,), jnp.int32),
        ),
        in_specs=[vmem, vmem, smem, smem, smem, vmem, vmem, anywhere, anywhere, vmem],
        out_specs=(anywhere, anywhere, vmem, vmem, smem),
        scratch_shapes=[
            pltpu.VMEM((POOL, *tile), f32),
            pltpu.VMEM((LINKS * RING, *tile), f32),
            pltpu.VMEM((LINKS * RING, *tile), f32),
            pltpu.VMEM((LINKS, 2, *tile), f32),
            pltpu.VMEM((children * depth, width), bf16),
            pltpu.VMEM((children * depth, width), bf16),
            pltpu.VMEM((children, width, depth), bf16),
            pltpu.VMEM((children, width, depth), bf16),
            pltpu.VMEM((depth, width), f32),
            pltpu.VMEM(diag_inverse.shape, f32),
            pltpu.VMEM((4, LEVELS, *parent_mean.shape), f32),
            pltpu.VMEM((2 * REACH - LEVELS + 2, LINKS, CHIPS, SLOTS), f32),
            pltpu.VMEM((CHIPS, SLOTS), jnp.int32),
            pltpu.VMEM((8, SLOTS), jnp.int32),
            pltpu.SMEM((8, SLOTS), jnp.int32),
            pltpu.SMEM((8, SLOTS), jnp.int32),
            dma((LINKS, 2)),
            dma((LINKS, RING)),
            dma((LINKS, RING)),
            dma((LINKS, RING)),
            dma((2,)),
            dma((LEVELS - 1,)),
            dma((LEVELS - 1,)),
            dma((4,)),
            dma,
            dma((children,)),
            dma((LINKS * RING,)),
            dma,
            pltpu.SemaphoreType.REGULAR((LINKS,)),
            pltpu.SemaphoreType.REGULAR((LINKS,)),
        ],
        compiler_params=pltpu.CompilerParams(
            collective_id=0, has_side_effects=True, vmem_limit_bytes=63 << 20
        ),
    )(
        owners,
        locals_,
        owners,
        locals_,
        config_weight,
        parent_tiles,
        parent_mean,
        factor_w,
        diag_inverse,
        own_mean,
    )


def any_reads(
    parent_tiles,
    parent_mean,
    factor_w,
    diag_inverse,
    own_mean,
    config_weight,
    need_owner,
    need_local,
):
    fronts = lax.axis_size("front")
    myself = lax.axis_index("front")
    stored = parent_tiles.shape[0]
    tile_size = parent_tiles.shape[1]
    child_count = factor_w.shape[0]
    own_cols = factor_w.shape[2]
    pattern = factor_w.shape[1] // tile_size
    need_count = child_count * pattern * pattern
    capacity = max(2, need_count // fronts + 1)
    owner_table = need_owner[:, 0].reshape(fronts, need_count)
    local_table = need_local.reshape(fronts, need_count)
    positions = jnp.arange(need_count, dtype=jnp.int32)
    earlier = positions[None, :] < positions[:, None]
    same_owner = owner_table[:, :, None] == owner_table[:, None, :]
    item_rank = jnp.sum(same_owner & earlier[None], axis=2)
    slot_range = jnp.arange(capacity, dtype=jnp.int32)
    outgoing = (owner_table[:, None, :] == myself) & (
        item_rank[:, None, :] == slot_range[None, :, None]
    )
    send_local = jnp.sum(jnp.where(outgoing, local_table[:, None, :], 0), axis=2).reshape(-1)
    send_mask = jnp.any(outgoing, axis=2).reshape(-1).astype(jnp.float32)
    my_owner = lax.dynamic_index_in_dim(owner_table, myself, 0, keepdims=False)
    my_rank = lax.dynamic_index_in_dim(item_rank, myself, 0, keepdims=False)
    my_local = lax.dynamic_index_in_dim(local_table, myself, 0, keepdims=False)
    arrival = my_owner * capacity + my_rank
    pair_index = jnp.arange(child_count * pattern, dtype=jnp.int32)
    diagonal_items = pair_index // pattern * pattern * pattern + pair_index % pattern * (
        pattern + 1
    )
    tile_buffer = (jnp.take(parent_tiles, send_local, axis=0) * send_mask[:, None, None]).reshape(
        fronts, capacity, tile_size, tile_size
    )
    received = lax.all_to_all(tile_buffer, "front", split_axis=0, concat_axis=0, tiled=True)
    item_tiles = jnp.take(
        received.reshape(fronts * capacity, tile_size, tile_size), arrival, axis=0
    )
    item_tiles = item_tiles.reshape(child_count, pattern, pattern, tile_size, tile_size)
    blocks = factor_w.reshape(child_count, pattern, tile_size, own_cols)
    sigma_pj = -jnp.einsum("cabij,cbjk->caik", item_tiles, blocks, precision=highest_precision)
    sigma_pj = sigma_pj.reshape(child_count, pattern * tile_size, own_cols)
    full_mean = lax.all_gather(parent_mean, "front", axis=0, tiled=True)
    parent_piece = jnp.take(full_mean, (my_owner * stored + my_local)[diagonal_items], axis=0)
    parent_piece = parent_piece.reshape(child_count, pattern * tile_size)
    sigma_jj = diag_inverse - jnp.einsum(
        "cpj,cpk->cjk", factor_w, sigma_pj, precision=highest_precision
    )
    variance = jnp.diagonal(sigma_jj, axis1=1, axis2=2)
    mean_value = own_mean - jnp.einsum(
        "cp,cpj->cj", parent_piece, factor_w, precision=highest_precision
    )
    weight = config_weight[0]
    return (sigma_pj, sigma_jj, weight * variance, weight * mean_value)


def finish_kernel(*refs):
    count = len(refs) // 2
    for source, result in zip(refs[:count], refs[count:]):
        result[...] = source[...]


def finish(*values):
    children, depth, width = values[0].shape
    parts = 2
    specs = (
        pl.BlockSpec((1, depth // parts, width), lambda step: (step // parts, step % parts, 0)),
        pl.BlockSpec((1, width // parts, width), lambda step: (step // parts, step % parts, 0)),
        pl.BlockSpec((children, width), lambda step: (0, 0)),
        pl.BlockSpec((children, width), lambda step: (0, 0)),
    )
    return pl.pallas_call(
        finish_kernel,
        grid=(children * parts,),
        out_shape=tuple(jax.ShapeDtypeStruct(value.shape, value.dtype) for value in values),
        in_specs=specs,
        out_specs=specs,
    )(*values)


def shards(
    parent_tiles,
    parent_mean,
    factor_w,
    diag_inverse,
    own_mean,
    config_weight,
    need_owner,
    need_local,
):
    operands = (parent_tiles, parent_mean, factor_w, diag_inverse, own_mean, config_weight)
    *outputs, fits = exchange(
        need_owner.reshape(CHIPS, -1), need_local.reshape(CHIPS, -1), *operands
    )
    return lax.cond(
        fits[0] > 0,
        lambda: tuple(finish(*outputs)),
        lambda: any_reads(*operands, need_owner, need_local),
    )


def solution(mesh):
    return jax.shard_map(
        shards,
        mesh=mesh,
        in_specs=(
            P(("cfg", "front"), None, None),
            P(("cfg", "front"), None),
            P(("cfg", "front"), None, None),
            P(("cfg", "front"), None, None),
            P(("cfg", "front"), None),
            P("cfg"),
            P(),
            P(),
        ),
        out_specs=(
            P(("cfg", "front"), None, None),
            P(("cfg", "front"), None, None),
            P(("cfg", "front"), None),
            P(("cfg", "front"), None),
        ),
        check_vma=False,
    )
```

```python
import functools

import jax
import jax.numpy as jnp
from jax import lax
from jax.experimental import pallas as pl
from jax.experimental.pallas import tpu as pltpu
from jax.sharding import PartitionSpec as P

highest_precision = lax.Precision.HIGHEST
MESH = pl.DeviceIdType.MESH

LEVELS = 8
CHIPS = 16
STORED = 8
CHIP_TILES = 16
SLOTS = 256
LINKS = 3
WINDOWS = 23
POOL = CHIP_TILES + 2 * LINKS * WINDOWS
RING = 4
REACH = 5
NONE = -1.0e6
ROUNDS = 2
EARLY = 10
STEEP = 0.03


def split_bf16(value):
    high = value.astype(jnp.bfloat16)
    return high, (value - high.astype(jnp.float32)).astype(jnp.bfloat16)


def dot3(left_high, left_low, right_high, right_low):
    def dot(left, right):
        return jnp.dot(left, right, preferred_element_type=jnp.float32)

    return dot(left_high, right_high) + (dot(left_high, right_low) + dot(left_low, right_high))


def swapped(value):
    return jnp.concatenate([value[LEVELS:], value[:LEVELS]], axis=0)


def turned(value, by):
    return jnp.concatenate(
        [pltpu.roll(value[:LEVELS], by, 0), pltpu.roll(value[LEVELS:], by, 0)], axis=0
    )


def most(value):
    return jnp.max(value, axis=0, keepdims=True)


def planner(slots, uses_ref):
    shape = (CHIPS, SLOTS)
    row = lax.broadcasted_iota(jnp.int32, shape, 0)
    lane = lax.broadcasted_iota(jnp.int32, shape, 1)
    one_lane = lax.broadcasted_iota(jnp.int32, (1, SLOTS), 1)
    chip_y, chip_z = row >> 3, row & 7
    owner_y, owner_z = lane >> 7, (lane >> 4) & 7
    need = jnp.zeros(shape, jnp.float32)
    for item in range(slots.shape[1]):
        need = jnp.where(slots[:, item : item + 1] == lane, 1.0, need)
    other_need = swapped(need)
    level_need = jnp.maximum(need, other_need) > 0.0
    ahead = ((chip_z - owner_z) & 7).astype(jnp.float32)
    behind = ((owner_z - chip_z) & 7).astype(jnp.float32)
    own_line = jnp.where(chip_y == owner_y, 1.0, 0.0)
    at_level = jnp.where(ahead == 0.0, 1.0, 0.0)
    at_owner = own_line * at_level
    needed_over = most(at_owner * other_need)
    ups, downs = [], []
    for option, cut in enumerate(range(LEVELS - 1 - REACH, REACH + 1)):
        up = most(jnp.where(level_need & (ahead <= cut), ahead, 0.0))
        down = most(jnp.where(level_need & (behind <= LEVELS - 1 - cut), behind, 0.0))
        ups.append(up)
        downs.append(down)
        uses_ref[option, 0] = jnp.where(ahead < up, 1.0, 0.0)
        uses_ref[option, 1] = jnp.where(behind < down, 1.0, 0.0)
        reached = jnp.where((ahead <= up) | (behind <= down), other_need, 0.0)
        uses_ref[option, 2] = reached * (1.0 - at_level * (1.0 - own_line))

    def sends(up, down, crosses):
        on_line = own_line * (1.0 - crosses) + (1.0 - own_line) * crosses
        reached = jnp.where((ahead <= up) | (behind <= down), on_line * other_need, 0.0)
        return (
            jnp.where(ahead < up, on_line, 0.0),
            jnp.where(behind < down, on_line, 0.0),
            reached * (1.0 - at_level * crosses) + at_owner * crosses,
            on_line,
        )

    def settle(step, carry, kept=None):
        choice, up, down, crosses = carry
        steep = jnp.where(step == 0, 0.0, STEEP)
        weights = [
            jnp.exp(steep * (jnp.sum(use, axis=1, keepdims=True) - 40.0))
            for use in sends(up, down, crosses)[:3]
        ]
        over = jnp.sum(at_owner * weights[2], axis=0, keepdims=True)
        best = jnp.full((1, SLOTS), 1.0e9, jnp.float32)
        chosen = [jnp.zeros((1, SLOTS), jnp.float32)] * 4
        for option in range(len(ups)):
            cost = sum(uses_ref[option, link] * weights[link] for link in range(LINKS))
            first = jnp.sum(cost[:LEVELS], axis=0, keepdims=True)
            second = jnp.sum(cost[LEVELS:], axis=0, keepdims=True)
            for side in range(2):
                total = jnp.where((one_lane < SLOTS // 2) == (side == 0), first, second)
                total = total + over * float(side)
                number = 2.0 * option + side
                total = jnp.where(choice == number, total - 0.1, total)
                if kept is not None:
                    kept_up, kept_down, kept_over = kept
                    if side == 0:
                        broken = kept_over * (1.0 - needed_over)
                        broken = broken + jnp.where(ups[option] == 0.0, kept_up, 0.0)
                        broken = broken + jnp.where(downs[option] == 0.0, kept_down, 0.0)
                    else:
                        broken = kept_up + kept_down
                    total = total + 1.0e4 * broken
                better = total < best
                best = jnp.where(better, total, best)
                values = (number, ups[option], downs[option], float(side))
                chosen = [jnp.where(better, v, c) for v, c in zip(values, chosen)]
        turn = ((one_lane & 15) == ((step - 1) & 15)) | (step == 0)
        return tuple(jnp.where(turn, c, old) for c, old in zip(chosen, carry))

    def ranked(carry):
        choice, up, down, crosses = carry
        send_up, send_down, send_over, on_line = sends(up, down, crosses)
        end_up = most(jnp.where(ahead == up, on_line * other_need, 0.0))
        end_down = most(jnp.where(behind == down, on_line * other_need, 0.0))
        longest = jnp.maximum(2.0 * up + 3.0 * end_up, 2.0 * down + 3.0 * end_down)
        rank_up = 2.0 * (up - ahead) + 3.0 * end_up + 2.0 * turned(other_need, LEVELS - 1)
        rank_down = 2.0 * (down - behind) + 3.0 * end_down + 2.0 * turned(other_need, 1)
        rank_over = jnp.where(at_owner * crosses > 0.0, longest + 2.0, 1.0)
        return (
            jnp.where(send_up > 0.0, rank_up * 256.0, NONE),
            jnp.where(send_down > 0.0, rank_down * 256.0, NONE),
            jnp.where(send_over > 0.0, rank_over * 256.0, NONE),
        )

    unchosen = (jnp.full((1, SLOTS), -1.0, jnp.float32),)
    unchosen = unchosen + (jnp.zeros((1, SLOTS), jnp.float32),) * 3
    at_start = (
        jnp.where(at_owner > 0.0, (255 - (lane & 15)).astype(jnp.float32), NONE),
        jnp.full(shape, NONE, jnp.float32),
        jnp.zeros(shape, jnp.int32),
    )
    return settle, ranked, unchosen, at_start


def schedule(w, carry):
    keys, held, coming, table = list(carry[:3]), carry[3], carry[4], carry[5]
    shape = held.shape
    lane = lax.broadcasted_iota(jnp.int32, shape, 1)
    arrives = []
    for link in range(LINKS):
        sent = jnp.full(shape, NONE, jnp.float32)
        for core in range(2):
            key = keys[link] + held
            key = jnp.where((((lane >> 3) & 1) == core) | (jnp.asarray(w) >= 2), key, NONE)
            top = jnp.max(key, axis=1, keepdims=True)
            hit = (key == top) & (top > 0.0)
            keys[link] = jnp.where(hit, NONE, keys[link])
            place = CHIP_TILES + link * 2 * WINDOWS + 2 * w + core
            sent = jnp.where(hit, jnp.asarray(255 - place).astype(jnp.float32), sent)
            found = jnp.where(top > 0.0, 255 - (top.astype(jnp.int32) & 255), 0)
            table = jnp.where(lane == 6 * w + 2 * link + core, found, table)
        arrives.append(sent)
    fresh = jnp.maximum(
        jnp.maximum(turned(arrives[0], 1), turned(arrives[1], LEVELS - 1)), swapped(arrives[2])
    )
    return (*keys, jnp.maximum(held, coming), fresh, table)


def exchange_kernel(
    owner_ref,
    local_ref,
    owner_item_ref,
    local_item_ref,
    weight_ref,
    tiles_ref,
    mean_ref,
    factor_ref,
    diag_ref,
    own_mean_ref,
    pj_ref,
    jj_ref,
    variance_ref,
    out_mean_ref,
    fits_ref,
    pool,
    land,
    passed,
    outgoing,
    high,
    low,
    turned_high,
    turned_low,
    stage,
    mine,
    means,
    uses,
    whole,
    rows_out,
    first_plan,
    plan,
    send_sem,
    land_sem,
    pass_send_sem,
    pass_sem,
    swap_sem,
    ring_send_sem,
    ring_sem,
    mean_sem,
    stage_sem,
    jj_sem,
    plan_sem,
    tiles_sem,
    credit,
    pass_credit,
):
    cfg, me = lax.axis_index("cfg"), lax.axis_index("front")
    y, z, core = me // 16, (me // 2) % 8, me % 2
    children = factor_ref.shape[0]

    def device(to_y, to_z, to_core):
        return (cfg, to_y * 16 + to_z * 2 + to_core)

    above = device(y, (z + 1) % 8, core)
    below = device(y, (z + 7) % 8, core)
    across = device(1 - y, z, core)
    partner = device(y, z, 1 - core)
    targets = (above, below, across)
    sources = (below, above, across)

    def signal(sem, to):
        pl.semaphore_signal(sem, inc=1, device_id=to, device_id_type=MESH)

    def remote(src, dst, sent, got, to):
        return pltpu.make_async_remote_copy(
            src_ref=src,
            dst_ref=dst,
            send_sem=sent,
            recv_sem=got,
            device_id=to,
            device_id_type=MESH,
        )

    def load_stage(child):
        return pltpu.make_async_copy(factor_ref.at[child], stage, stage_sem)

    jj_load = pltpu.make_async_copy(diag_ref, jj_ref, jj_sem.at[0])
    tiles_load = pltpu.make_async_copy(tiles_ref, mine, tiles_sem)
    tiles_load.start()
    load_stage(0).start()
    jj_load.start()
    barrier = pltpu.get_barrier_semaphore()
    for neighbour in (above, below, across, partner):
        signal(barrier, neighbour)
    line = y * 2 + core
    means[line, z] = mean_ref[...]
    settle, ranked, unchosen, at_start = planner(owner_ref[...] * STORED + local_ref[...], uses)
    chosen = settle(0, unchosen)
    first_keys = ranked(chosen)
    after = schedule(0, (*first_keys, *at_start))
    gone = [(old > 0.0) & (new < 0.0) for old, new in zip(first_keys, after)]
    kept = [most(jnp.where(sent, 1.0, 0.0)) for sent in gone]

    def own_row(at, values):
        whole[...] = values
        rows_out[at : at + 1, :] = whole[pl.ds(me // 2, 1), :]

    own_row(0, after[5])
    first_copy = pltpu.make_async_copy(rows_out, first_plan, plan_sem)
    first_copy.start()

    def resettle(step, carry):
        return settle(step, carry, kept)

    chosen = lax.fori_loop(1, 1 + EARLY, resettle, chosen)
    first_copy.wait()
    tiles_load.wait()
    pl.semaphore_wait(barrier, 4)

    own = pl.ds(core * STORED, STORED)
    swap = remote(mine, pool.at[own], swap_sem.at[0], swap_sem.at[1], partner)

    def ring(step):
        block = means.at[line, (z + 8 - step) % 8]
        return remote(block, block, ring_send_sem.at[step], ring_sem.at[step], above)

    def send(w, link):
        return remote(
            outgoing.at[link, w % 2],
            land.at[link * RING + w % RING],
            send_sem.at[link, w % 2],
            land_sem.at[link, w % RING],
            targets[link],
        )

    def hand_over(v, link):
        place = link * RING + v % RING
        return remote(
            land.at[place],
            passed.at[place],
            pass_send_sem.at[link, v % RING],
            pass_sem.at[link, v % RING],
            partner,
        )

    def planned(table, w, link):
        return jnp.clip(table[0, 6 * w + 2 * link + core], 0, POOL - 1)

    def send_own(w, table):
        for link in range(LINKS):
            outgoing[link, w] = mine[planned(table, w, link) % STORED]
            send(w, link).start()

    send_own(0, first_plan)
    swap.start()
    ring(0).start()
    chosen = lax.fori_loop(1 + EARLY, 1 + 16 * ROUNDS, resettle, chosen)
    keys = [jnp.where(sent, NONE, key) for sent, key in zip(gone, ranked(chosen))]
    routes = schedule(1, (*keys, *after[3:]))
    own_row(0, routes[5])
    plan_copy = pltpu.make_async_copy(rows_out, plan, plan_sem)
    plan_copy.start()
    plan_copy.wait()
    send_own(1, plan)

    def keep(tile, carry):
        pool[core * STORED + tile] = mine[tile]
        return carry

    lax.fori_loop(0, STORED, keep, 0)
    key_up, key_down, key_over, held, coming, table = lax.fori_loop(2, WINDOWS, schedule, routes)
    held = jnp.maximum(held, coming)
    own_row(0, table)
    own_row(1, jnp.where(held >= 0.0, 255 - held.astype(jnp.int32), 0))
    plan_copy.start()
    left = jnp.maximum(jnp.maximum(key_up, key_down), key_over)
    fits_ref[0] = jnp.where(jnp.max(left) > 0.0, 0, 1)
    plan_copy.wait()
    swap.wait()

    def take(v):
        for link in range(LINKS):
            send(v, link).wait_recv()

            @pl.when(v >= RING)
            def _():
                pl.semaphore_wait(pass_credit.at[link], 1)

            hand_over(v, link).start()
        for link in range(LINKS):
            place = CHIP_TILES + link * 2 * WINDOWS + 2 * v
            pool[place + core] = land[link * RING + v % RING]
        for link in range(LINKS):
            hand_over(v, link).wait_send()

            @pl.when(v < WINDOWS - RING)
            def _():
                signal(credit.at[link], sources[link])

        for link in range(LINKS):
            hand_over(v, link).wait_recv()
            place = CHIP_TILES + link * 2 * WINDOWS + 2 * v
            pool[place + 1 - core] = passed[link * RING + v % RING]

            @pl.when(v < WINDOWS - RING)
            def _():
                signal(pass_credit.at[link], partner)

    both = means.at[pl.ds(y * 2, 2)]
    line_swap = remote(means.at[line], means.at[line], mean_sem.at[0], mean_sem.at[1], partner)
    mean_swap = remote(both, both, mean_sem.at[2], mean_sem.at[3], across)

    def slot_of(item):
        at = core * (children * 16) + item
        return owner_item_ref[me // 2, at] * STORED + local_item_ref[me // 2, at]

    weight = weight_ref[0]

    def weigh_mean(child):
        total = jnp.zeros((16, 256), jnp.float32)
        for a in range(4):
            slot = slot_of(child * 16 + a * 5)
            slot_line = slot // 128 * 2 + slot // 8 % 2
            piece = means[slot_line, slot // 16 % 8, pl.ds(slot % 8, 1), :]
            piece_high, piece_low = split_bf16(jnp.broadcast_to(piece, (16, 256)))
            rows = pl.ds(child * 1024 + a * 256, 256)
            total += dot3(piece_high, piece_low, high[rows, :], low[rows, :])
        value = own_mean_ref[pl.ds(child, 1), :] - total[0:1]
        out_mean_ref[pl.ds(child, 1), :] = weight * value

    def window(w, carry):
        take(w - 2)
        for link in range(LINKS):
            send(w, link).wait_send()
            outgoing[link, w % 2] = pool[planned(plan, w, link)]

            @pl.when(w >= RING)
            def _():
                pl.semaphore_wait(credit.at[link], 1)

            send(w, link).start()

        @pl.when(w < 9)
        def _():
            ring(w - 2).wait()

            @pl.when(w < 8)
            def _():
                ring(w - 1).start()

        @pl.when(w == 9)
        def _():
            line_swap.start()

        @pl.when(w == 10)
        def _():
            line_swap.wait()
            mean_swap.start()

        @pl.when(w == 11)
        def _():
            mean_swap.wait()

        @pl.when((w >= 12) & (w < 12 + children))
        def _():
            weigh_mean(w - 12)

        @pl.when((w >= 3) & (w < 3 + children))
        def _():
            child = w - 3
            load_stage(child).wait()
            for b in range(4):
                rows = pl.ds(child * 1024 + b * 256, 256)
                block = stage[b * 256 : (b + 1) * 256, :]
                high[rows, :], low[rows, :] = split_bf16(block)
                cols = pl.ds(b * 256, 256)
                block_t = block.T
                turned_high[child, :, cols], turned_low[child, :, cols] = split_bf16(block_t)

            @pl.when(child + 1 < children)
            def _():
                load_stage(child + 1).start()

        return carry

    lax.fori_loop(2, WINDOWS, window, 0)
    take(WINDOWS - 2)
    take(WINDOWS - 1)
    for w in range(WINDOWS - 2, WINDOWS):
        for link in range(LINKS):
            send(w, link).wait_send()
    jj_load.wait()

    rows_at = lax.broadcasted_iota(jnp.int32, (256, 256), 0)
    cols_at = lax.broadcasted_iota(jnp.int32, (256, 256), 1)

    def front(child, carry):
        def pattern_row(a, carry):
            total = jnp.zeros((256, 256), jnp.float32)
            for b in range(4):
                item = jnp.clip(plan[1, slot_of(child * 16 + a * 4 + b)], 0, POOL - 1)
                tile_high, tile_low = split_bf16(pool[item])
                rows = pl.ds(child * 1024 + b * 256, 256)
                total += dot3(tile_high, tile_low, high[rows, :], low[rows, :])
            block = -total
            pj_ref[child, pl.ds(pl.multiple_of(a * 256, 256), 256), :] = block
            block_high, block_low = split_bf16(block)
            cols = pl.ds(pl.multiple_of(a * 256, 256), 256)
            jj_ref[child] -= dot3(
                turned_high[child, :, cols], turned_low[child, :, cols], block_high, block_low
            )
            return carry

        lax.fori_loop(0, 4, pattern_row, 0)
        diagonal = jnp.where(rows_at == cols_at, jj_ref[child], 0.0)
        variance_ref[pl.ds(child, 1), :] = weight * jnp.sum(diagonal, axis=0, keepdims=True)
        return carry

    lax.fori_loop(0, children, front, 0)


def exchange(owners, locals_, parent_tiles, parent_mean, factor_w, diag_inverse, own_mean, config_weight):
    tile = parent_tiles.shape[1:]
    children, depth, width = factor_w.shape
    vmem = pl.BlockSpec(memory_space=pltpu.VMEM)
    smem = pl.BlockSpec(memory_space=pltpu.SMEM)
    anywhere = pl.BlockSpec(memory_space=pl.ANY)
    dma = pltpu.SemaphoreType.DMA
    f32, bf16 = jnp.float32, jnp.bfloat16
    return pl.pallas_call(
        exchange_kernel,
        out_shape=(
            pltpu.VMEM(factor_w.shape, f32),
            jax.ShapeDtypeStruct(diag_inverse.shape, f32),
            jax.ShapeDtypeStruct(own_mean.shape, f32),
            jax.ShapeDtypeStruct(own_mean.shape, f32),
            jax.ShapeDtypeStruct((1,), jnp.int32),
        ),
        in_specs=[vmem, vmem, smem, smem, smem, anywhere, vmem, anywhere, anywhere, vmem],
        out_specs=(vmem, vmem, vmem, vmem, smem),
        scratch_shapes=[
            pltpu.VMEM((POOL, *tile), f32),
            pltpu.VMEM((LINKS * RING, *tile), f32),
            pltpu.VMEM((LINKS * RING, *tile), f32),
            pltpu.VMEM((LINKS, 2, *tile), f32),
            pltpu.VMEM((children * depth, width), bf16),
            pltpu.VMEM((children * depth, width), bf16),
            pltpu.VMEM((children, width, depth), bf16),
            pltpu.VMEM((children, width, depth), bf16),
            pltpu.VMEM((depth, width), f32),
            pltpu.VMEM((STORED, *tile), f32),
            pltpu.VMEM((4, LEVELS, *parent_mean.shape), f32),
            pltpu.VMEM((2 * REACH - LEVELS + 2, LINKS, CHIPS, SLOTS), f32),
            pltpu.VMEM((CHIPS, SLOTS), jnp.int32),
            pltpu.VMEM((8, SLOTS), jnp.int32),
            pltpu.SMEM((8, SLOTS), jnp.int32),
            pltpu.SMEM((8, SLOTS), jnp.int32),
            dma((LINKS, 2)),
            dma((LINKS, RING)),
            dma((LINKS, RING)),
            dma((LINKS, RING)),
            dma((2,)),
            dma((LEVELS - 1,)),
            dma((LEVELS - 1,)),
            dma((4,)),
            dma,
            dma((children,)),
            dma,
            dma,
            pltpu.SemaphoreType.REGULAR((LINKS,)),
            pltpu.SemaphoreType.REGULAR((LINKS,)),
        ],
        compiler_params=pltpu.CompilerParams(
            collective_id=0, has_side_effects=True, vmem_limit_bytes=58 << 20
        ),
    )(
        owners,
        locals_,
        owners,
        locals_,
        config_weight,
        parent_tiles,
        parent_mean,
        factor_w,
        diag_inverse,
        own_mean,
    )


def any_reads(
    parent_tiles,
    parent_mean,
    factor_w,
    diag_inverse,
    own_mean,
    config_weight,
    need_owner,
    need_local,
):
    fronts = lax.axis_size("front")
    myself = lax.axis_index("front")
    stored = parent_tiles.shape[0]
    tile_size = parent_tiles.shape[1]
    child_count = factor_w.shape[0]
    own_cols = factor_w.shape[2]
    pattern = factor_w.shape[1] // tile_size
    need_count = child_count * pattern * pattern
    capacity = max(2, need_count // fronts + 1)
    owner_table = need_owner[:, 0].reshape(fronts, need_count)
    local_table = need_local.reshape(fronts, need_count)
    positions = jnp.arange(need_count, dtype=jnp.int32)
    earlier = positions[None, :] < positions[:, None]
    same_owner = owner_table[:, :, None] == owner_table[:, None, :]
    item_rank = jnp.sum(same_owner & earlier[None], axis=2)
    slot_range = jnp.arange(capacity, dtype=jnp.int32)
    outgoing = (owner_table[:, None, :] == myself) & (
        item_rank[:, None, :] == slot_range[None, :, None]
    )
    send_local = jnp.sum(jnp.where(outgoing, local_table[:, None, :], 0), axis=2).reshape(-1)
    send_mask = jnp.any(outgoing, axis=2).reshape(-1).astype(jnp.float32)
    my_owner = lax.dynamic_index_in_dim(owner_table, myself, 0, keepdims=False)
    my_rank = lax.dynamic_index_in_dim(item_rank, myself, 0, keepdims=False)
    my_local = lax.dynamic_index_in_dim(local_table, myself, 0, keepdims=False)
    arrival = my_owner * capacity + my_rank
    pair_index = jnp.arange(child_count * pattern, dtype=jnp.int32)
    diagonal_items = pair_index // pattern * pattern * pattern + pair_index % pattern * (
        pattern + 1
    )
    tile_buffer = (jnp.take(parent_tiles, send_local, axis=0) * send_mask[:, None, None]).reshape(
        fronts, capacity, tile_size, tile_size
    )
    received = lax.all_to_all(tile_buffer, "front", split_axis=0, concat_axis=0, tiled=True)
    item_tiles = jnp.take(
        received.reshape(fronts * capacity, tile_size, tile_size), arrival, axis=0
    )
    item_tiles = item_tiles.reshape(child_count, pattern, pattern, tile_size, tile_size)
    blocks = factor_w.reshape(child_count, pattern, tile_size, own_cols)
    sigma_pj = -jnp.einsum("cabij,cbjk->caik", item_tiles, blocks, precision=highest_precision)
    sigma_pj = sigma_pj.reshape(child_count, pattern * tile_size, own_cols)
    full_mean = lax.all_gather(parent_mean, "front", axis=0, tiled=True)
    parent_piece = jnp.take(full_mean, (my_owner * stored + my_local)[diagonal_items], axis=0)
    parent_piece = parent_piece.reshape(child_count, pattern * tile_size)
    sigma_jj = diag_inverse - jnp.einsum(
        "cpj,cpk->cjk", factor_w, sigma_pj, precision=highest_precision
    )
    variance = jnp.diagonal(sigma_jj, axis1=1, axis2=2)
    mean_value = own_mean - jnp.einsum(
        "cp,cpj->cj", parent_piece, factor_w, precision=highest_precision
    )
    weight = config_weight[0]
    return (sigma_pj, sigma_jj, weight * variance, weight * mean_value)


def finish_kernel(pj_ref, jj_ref, variance_ref, mean_ref, *refs):
    pj_out, jj_out, variance_out, mean_out, sems = refs
    copies = [
        pltpu.make_async_copy(pj_ref, pj_out, sems.at[0]),
        pltpu.make_async_copy(jj_ref, jj_out, sems.at[1]),
    ]
    for copy in copies:
        copy.start()
    variance_out[...] = variance_ref[...]
    mean_out[...] = mean_ref[...]
    for copy in copies:
        copy.wait()


def finish(*values):
    vmem = pl.BlockSpec(memory_space=pltpu.VMEM)
    anywhere = pl.BlockSpec(memory_space=pl.ANY)
    return pl.pallas_call(
        finish_kernel,
        out_shape=tuple(jax.ShapeDtypeStruct(value.shape, value.dtype) for value in values),
        in_specs=[vmem] * 4,
        out_specs=(anywhere, anywhere, vmem, vmem),
        scratch_shapes=[pltpu.SemaphoreType.DMA((2,))],
    )(pltpu.with_memory_space_constraint(values[0], pltpu.VMEM), *values[1:])


def shards(
    parent_tiles,
    parent_mean,
    factor_w,
    diag_inverse,
    own_mean,
    config_weight,
    need_owner,
    need_local,
):
    operands = (parent_tiles, parent_mean, factor_w, diag_inverse, own_mean, config_weight)
    *outputs, fits = exchange(
        need_owner.reshape(CHIPS, -1), need_local.reshape(CHIPS, -1), *operands
    )
    done = tuple(finish(*outputs))
    return lax.cond(
        fits[0] > 0,
        lambda: done,
        lambda: any_reads(*operands, need_owner, need_local),
    )


def solution(mesh):
    return jax.shard_map(
        shards,
        mesh=mesh,
        in_specs=(
            P(("cfg", "front"), None, None),
            P(("cfg", "front"), None),
            P(("cfg", "front"), None, None),
            P(("cfg", "front"), None, None),
            P(("cfg", "front"), None),
            P("cfg"),
            P(),
            P(),
        ),
        out_specs=(
            P(("cfg", "front"), None, None),
            P(("cfg", "front"), None, None),
            P(("cfg", "front"), None),
            P(("cfg", "front"), None),
        ),
        check_vma=False,
    )
```
